32 devices in a mesh: dp: 4 (over z), seq: 2 (over x), mp: 4 (over y, core).
Axes of the slice: x: 2, y: 2, z: 4, core: 2. Of those that a mesh axis runs over, the one named last changes fastest.
Arguments:
- queries: bfloat16 [4, 2, 4, 64, 4096], P('dp', 'seq', None, None, 'mp'), may hold values from -8 to 8
- key_vectors: bfloat16 [4, 2, 4, 64, 4096], P('dp', 'seq', None, None, 'mp'), may hold values from -8 to 8
- value_rows: bfloat16 [4, 2, 4, 64, 4096], P('dp', 'seq', None, None, 'mp'), may hold values from -6 to 6
- upstream: bfloat16 [4, 2, 4, 64, 4096], P('dp', 'seq', None, None, 'mp'), may hold values from -6 to 6
- segments: int32 [4, 512], P('dp'), may hold values from 0 to 7, never falling along the last dimension, each value on 1 to 128 neighbouring positions
- losses: float32 [4, 8], P('dp'), may hold values from 0.3 to 13.5
- offsets: int32 [4], replicated, may hold values from 0 to 3, each once
Outputs:
- query_grad: bfloat16 [4, 2, 4, 64, 4096], P('dp', 'seq', None, None, 'mp')
- key_grad: bfloat16 [4, 2, 4, 64, 4096], P('dp', 'seq', None, None, 'mp')
- value_grad: bfloat16 [4, 2, 4, 64, 4096], P('dp', 'seq', None, None, 'mp')
The draws below stay inside these ranges and needn't reach their ends.
Inputs may be any that keep to these rules, and one draw needn't show every extreme that they name: `offsets`: every value from 0 to 3 occurs exactly once. `segments`: within a pack ids never fall and every id from 0 to 7 occurs; an image has at most 128 tokens and some image exactly that many.
All inputs are finite; a program needn't handle non-finite values.
Results may differ from the reference program's by a relative error of at most 0.012.
Values may be sent and summed in bfloat16 or wider, within the bound.
A program may use at most 64 MiB of HBM per device.

```python
import math
import jax
import jax.numpy as jnp
import numpy as np
from jax import lax

HEADS = 32
HD = 128
IMG_PACK = 8
PIECE_DEV = 4
PIECE_ROWS = 64
PACK = 512
N_DP = 4
N_SEQ = 2


def drawn_rows(key, salt):
    shape = (N_DP, N_SEQ, PIECE_DEV, PIECE_ROWS, HEADS * HD)
    return jnp.clip(jax.random.normal(jax.random.fold_in(key, salt), shape, jnp.float32), -4.0, 4.0)


def draw_queries(key, part):
    result = drawn_rows(key, 11)
    return result.astype(jnp.bfloat16)


def draw_key_vectors(key, part):
    result = drawn_rows(key, 12)
    return result.astype(jnp.bfloat16)


def draw_losses(key, part):
    rank = jnp.arange(N_DP, dtype=jnp.float32).reshape(N_DP, 1)
    rising = 1.0 + 2.0 * rank / (N_DP - 1)
    logs = jax.random.uniform(key, (N_DP, IMG_PACK), jnp.float32, jnp.log(0.3), jnp.log(1.5))
    return jnp.exp(logs) * rising


def block_scale(key, extent, pieces, least, largest):
    level = 1.0
    for position, parts in pieces:
        steps = jax.random.uniform(jax.random.fold_in(jax.random.fold_in(key, 6), position), (parts,), jnp.float32, least / len(pieces), largest / len(pieces))
        level = level * jnp.repeat(jnp.exp(steps), extent[position] // parts).reshape((-1,) + (1,) * (len(extent) - 1 - position))
    return level


def length_profile(number_of, total, most, slope):
    weights = [(1 << 20) // math.isqrt(rank ** slope) + 1 for rank in range(2, number_of + 1)]
    rest, holding = total - most - (number_of - 1), [1] * (number_of - 1)
    while rest > 0:
        movable = [i for i in range(number_of - 1) if holding[i] < most]
        whole, left = sum([weights[i] for i in movable]), rest
        for i in movable:
            more = min(most - holding[i], max(1, left * weights[i] // whole), rest)
            holding[i] = holding[i] + more
            rest = rest - more
    return np.array([most] + holding)


def ragged_sizes(stream_key, number_of, total, reach, skew):
    if number_of == 2:
        one = jax.random.randint(stream_key, (), max(1, total - reach), min(reach, total - 1) + 1)
        return jnp.stack([one, total - one])
    sizes = jnp.asarray(length_profile(number_of, total, reach, skew), jnp.int32)
    couples = (number_of - 1) // 2
    source_of, receiver = sizes[1:1 + 2 * couples:2], sizes[2:2 + 2 * couples:2]
    margin = jnp.minimum(source_of - 1, reach - receiver)
    shifted = jax.random.randint(jax.random.fold_in(stream_key, 1), (couples,), 0, 1 << 20) % (margin + 1)
    sizes = sizes.at[1:1 + 2 * couples:2].set(source_of - shifted).at[2:2 + 2 * couples:2].set(receiver + shifted)
    return sizes[jax.random.permutation(jax.random.fold_in(stream_key, 2), number_of)]


def gaussian(stream_key, dims, deviation, reach, pieces=(), kind=jnp.bfloat16):
    level = block_scale(stream_key, dims, pieces, -0.22, 0.18) if pieces else 1.0
    values = jax.random.normal(stream_key, dims, jnp.float32) * deviation * level
    return jnp.minimum(jnp.maximum(values, -reach), reach).astype(kind)


def setup_inputs(seed: int = 0) -> dict:
    arg_keys = jax.random.split(jax.random.key(seed), 8)
    return {
        "queries": draw_queries(jax.random.fold_in(arg_keys[7], 71), 0),
        "key_vectors": draw_key_vectors(jax.random.fold_in(arg_keys[7], 71), 0),
        "value_rows": gaussian(arg_keys[2], (N_DP, N_SEQ, PIECE_DEV, PIECE_ROWS, HEADS * HD), 1.0, 6.0, ((0, 4), (1, 2), (4, 4))),
        "upstream": gaussian(arg_keys[3], (N_DP, N_SEQ, PIECE_DEV, PIECE_ROWS, HEADS * HD), 1.0, 6.0, ((0, 4), (1, 2), (4, 4))),
        "segments": jax.vmap(lambda own: jnp.searchsorted(jnp.cumsum(ragged_sizes(own, IMG_PACK, PACK, PACK // 4, 1)), jnp.arange(PACK), side="right"))(jax.random.split(arg_keys[4], N_DP)).reshape((N_DP, PACK)).astype(jnp.int32),
        "losses": draw_losses(jax.random.fold_in(arg_keys[7], 71), 0),
        "offsets": jax.random.permutation(arg_keys[6], N_DP).astype(jnp.int32),
    }


def pack_backward(queries_p, keys_p, values_p, upstream_p, image_ids, token_weight):
    factor = HD ** -0.5
    grad_out = (token_weight[:, None, None] * upstream_p.astype(jnp.float32)).astype(jnp.bfloat16)
    q_full = queries_p.astype(jnp.float32)
    k_full = keys_p.astype(jnp.float32)
    v_full = values_p.astype(jnp.float32)
    g_full = grad_out.astype(jnp.float32)
    same_image = image_ids[:, None] == image_ids[None, :]
    scores = jnp.einsum("thd,uhd->htu", q_full, k_full) * factor
    masked = jnp.where(same_image[None], scores, -1e30)
    row_top = jnp.max(masked, axis=2, keepdims=True)
    exponent = jnp.where(same_image[None], jnp.exp(masked - row_top), 0.0)
    attention = exponent / jnp.sum(exponent, axis=2, keepdims=True)
    attention_low = attention.astype(jnp.bfloat16)
    grad_attention = jnp.einsum("thd,uhd->htu", g_full, v_full)
    row_inner = jnp.sum(attention * grad_attention, axis=2, keepdims=True)
    grad_scores = (attention * (grad_attention - row_inner) * factor).astype(jnp.bfloat16)
    grad_full = grad_scores.astype(jnp.float32)
    query_out = jnp.einsum("htu,uhd->thd", grad_full, k_full).astype(jnp.bfloat16)
    key_out = jnp.einsum("htu,thd->uhd", grad_full, q_full).astype(jnp.bfloat16)
    value_out = jnp.einsum("htu,thd->uhd", attention_low.astype(jnp.float32), g_full).astype(jnp.bfloat16)
    return query_out, key_out, value_out


def reference(queries, key_vectors, value_rows, upstream, segments, losses, offsets):
    loss_mean = jnp.mean(losses)
    image_weight = 2.0 / (1.0 + jnp.exp(losses - loss_mean))
    token_weight = jnp.take_along_axis(image_weight, segments, axis=1)
    dp_index = jnp.arange(N_DP, dtype=jnp.int32)[:, None]
    group_index = jnp.arange(PIECE_DEV, dtype=jnp.int32)[None, :]
    sources = ((dp_index - offsets[None, :]) % N_DP).astype(jnp.int32)
    targets = ((dp_index + offsets[None, :]) % N_DP).astype(jnp.int32)

    def to_pack(array):
        moved = array[sources, :, group_index]
        moved = jnp.transpose(moved, (0, 2, 1, 3, 4))
        return moved.reshape(N_DP, PACK, HEADS, HD)

    def from_pack(array):
        shaped = array.reshape(N_DP, N_SEQ, PIECE_DEV, PIECE_ROWS, HEADS * HD)
        moved = shaped[targets, :, group_index]
        return jnp.transpose(moved, (0, 2, 1, 3, 4))

    packed = (to_pack(queries), to_pack(key_vectors), to_pack(value_rows), to_pack(upstream))

    def one_pack(items):
        return pack_backward(items[0], items[1], items[2], items[3], items[4], items[5])

    query_out, key_out, value_out = lax.map(one_pack, (packed[0], packed[1], packed[2], packed[3], segments, token_weight))
    return from_pack(query_out), from_pack(key_out), from_pack(value_out)
```

```python
import functools
import math

import jax
import jax.numpy as jnp
from jax import lax
from jax.experimental import pallas as pl
from jax.experimental.pallas import tpu as pltpu
from jax.sharding import PartitionSpec as P

HD = 128


def for_sending(shard):

    def short(part):
        return part.astype(jnp.bfloat16) if part.dtype == jnp.float32 else part

    return jax.tree.map(short, shard)


def picked(block, slots):
    chosen = (slots[:, None] == jnp.arange(block.shape[0])[None, :]).astype(jnp.bfloat16)
    return jnp.einsum("jn,nrc->jrc", chosen, block, preferred_element_type=jnp.float32).astype(
        jnp.bfloat16
    )


def softmax_grads(q_rows, k_rows, v_rows, d_rows, image_ids):
    total_rows = q_rows.shape[0]
    block_rows = min(512, total_rows)
    factor = q_rows.shape[1] ** (-0.5)
    key_total = jnp.zeros(k_rows.shape, jnp.float32)
    value_total = jnp.zeros(v_rows.shape, jnp.float32)
    query_pieces = []
    for start_row in range(0, total_rows, block_rows):
        q_block = q_rows[start_row : start_row + block_rows]
        d_block = d_rows[start_row : start_row + block_rows]
        same_image = image_ids[start_row : start_row + block_rows, None] == image_ids[None, :]
        scores = (
            jnp.einsum("td,ud->tu", q_block, k_rows, preferred_element_type=jnp.float32) * factor
        )
        masked = jnp.where(same_image, scores, -1e30)
        row_top = jnp.max(masked, axis=1, keepdims=True)
        exponent = jnp.exp(masked - row_top)
        attention = exponent / jnp.sum(exponent, axis=1, keepdims=True)
        grad_attention = jnp.einsum(
            "td,ud->tu", d_block, v_rows, preferred_element_type=jnp.float32
        )
        row_inner = jnp.sum(attention * grad_attention, axis=1, keepdims=True)
        grad_scores = (attention * (grad_attention - row_inner) * factor).astype(jnp.bfloat16)
        query_pieces.append(
            jnp.einsum("tu,ud->td", grad_scores, k_rows, preferred_element_type=jnp.float32).astype(
                jnp.bfloat16
            )
        )
        key_total = key_total + jnp.einsum(
            "tu,td->ud", grad_scores, q_block, preferred_element_type=jnp.float32
        )
        value_total = value_total + jnp.einsum(
            "tu,td->ud", attention.astype(jnp.bfloat16), d_block, preferred_element_type=jnp.float32
        )
    return (
        jnp.concatenate(query_pieces, axis=0),
        key_total.astype(jnp.bfloat16),
        value_total.astype(jnp.bfloat16),
    )


def plain_shards(queries, key_vectors, value_rows, upstream, segments, losses, offsets):
    pieces = queries.shape[2]
    piece_rows = queries.shape[3]
    columns = queries.shape[4]
    local_rows = pieces * piece_rows
    dp_count = lax.axis_size("dp")
    seq_count = lax.axis_size("seq")
    position = lax.axis_index("dp")
    dp_slots = jnp.arange(dp_count, dtype=jnp.int32)
    loss_sum = lax.psum(jnp.sum(losses), "dp")
    loss_mean = loss_sum / (losses.shape[1] * dp_count)
    image_weight = 2.0 / (1.0 + jnp.exp(losses[0] - loss_mean))
    image_ids = segments[0]
    image_slots = jnp.arange(losses.shape[1], dtype=jnp.int32)
    token_weight = jnp.sum(
        jnp.where(image_ids[:, None] == image_slots[None, :], image_weight[None, :], 0.0), axis=1
    )
    local_parts = tuple(
        (
            array.reshape(pieces, piece_rows, columns)
            for array in (queries, key_vectors, value_rows, upstream)
        )
    )
    targets = (position + offsets) % dp_count
    select = (targets[None, :] == dp_slots[:, None]).astype(jnp.bfloat16)
    outgoing = tuple(
        (
            jnp.einsum("nj,jrc->nrc", select, block, preferred_element_type=jnp.float32).astype(
                jnp.bfloat16
            )
            for block in local_parts
        )
    )
    incoming = (
        lax.all_to_all(outgoing[0], "dp", split_axis=0, concat_axis=0, tiled=True),
        lax.all_to_all(outgoing[1], "dp", split_axis=0, concat_axis=0, tiled=True),
        lax.all_to_all(outgoing[2], "dp", split_axis=0, concat_axis=0, tiled=True),
        lax.all_to_all(outgoing[3], "dp", split_axis=0, concat_axis=0, tiled=True),
    )
    sources = (position - offsets) % dp_count
    arrived = tuple((picked(block, sources) for block in incoming))
    heads_each = columns // (seq_count * HD)
    grouped = tuple((block.reshape(local_rows, seq_count, heads_each, HD) for block in arrived))
    q_all = lax.all_to_all(grouped[0], "seq", split_axis=1, concat_axis=0, tiled=True)[:, 0]
    k_all = lax.all_to_all(grouped[1], "seq", split_axis=1, concat_axis=0, tiled=True)[:, 0]
    v_all = lax.all_to_all(grouped[2], "seq", split_axis=1, concat_axis=0, tiled=True)[:, 0]
    grad_out = (
        token_weight[:, None, None]
        * lax.all_to_all(grouped[3], "seq", split_axis=1, concat_axis=0, tiled=True)[:, 0].astype(
            jnp.float32
        )
    ).astype(jnp.bfloat16)
    grads = jax.vmap(softmax_grads, in_axes=(1, 1, 1, 1, None), out_axes=1)(
        q_all, k_all, v_all, grad_out, image_ids
    )
    results = tuple((item[:, None] for item in grads))
    returned = (
        lax.all_to_all(for_sending(results[0]), "seq", split_axis=0, concat_axis=1, tiled=True),
        lax.all_to_all(for_sending(results[1]), "seq", split_axis=0, concat_axis=1, tiled=True),
        lax.all_to_all(for_sending(results[2]), "seq", split_axis=0, concat_axis=1, tiled=True),
    )
    back_parts = tuple((block.reshape(pieces, piece_rows, columns) for block in returned))
    anchors = (position - offsets) % dp_count
    select_back = (anchors[None, :] == dp_slots[:, None]).astype(jnp.bfloat16)
    outgoing_back = tuple(
        (
            jnp.einsum(
                "nj,jrc->nrc", select_back, block, preferred_element_type=jnp.float32
            ).astype(jnp.bfloat16)
            for block in back_parts
        )
    )
    incoming_back = (
        lax.all_to_all(outgoing_back[0], "dp", split_axis=0, concat_axis=0, tiled=True),
        lax.all_to_all(outgoing_back[1], "dp", split_axis=0, concat_axis=0, tiled=True),
        lax.all_to_all(outgoing_back[2], "dp", split_axis=0, concat_axis=0, tiled=True),
    )
    destinations = (position + offsets) % dp_count
    finished = tuple((picked(block, destinations) for block in incoming_back))
    return tuple((block.reshape(1, 1, pieces, piece_rows, columns) for block in finished))


MESH = pl.DeviceIdType.MESH


def dot_nt(a, b):
    return lax.dot_general(a, b, (((1,), (1,)), ((), ())), preferred_element_type=jnp.float32)


def dot_tn(a, b):
    return lax.dot_general(a, b, (((0,), (0,)), ((), ())), preferred_element_type=jnp.float32)


def exchange_kernel(
    n_dp,
    n_seq,
    pieces,
    rows,
    heads_each,
    images,
    offsets_ref,
    segments_ref,
    losses_ref,
    q_ref,
    k_ref,
    v_ref,
    d_ref,
    dq_ref,
    dk_ref,
    dv_ref,
    *scratch,
):
    (send, recv, back_send, loss_send, loss_recv, ids_row, weight) = scratch[:7]
    back_recv = scratch[7 : 7 + heads_each]
    send_sem, recv_sem, back_send_sem, back_recv_sem, loss_send_sem, loss_recv_sem = scratch[
        7 + heads_each :
    ]
    z = lax.axis_index("dp")
    x = lax.axis_index("seq")
    me = z * n_seq + x
    parts = n_dp * n_seq
    total = parts * rows
    factor = HD**-0.5
    log2e = math.log2(math.e)

    dp_shifts = sorted(range(n_dp), key=lambda s: -min(s, n_dp - s))
    all_shifts = [(a, b) for a in dp_shifts for b in reversed(range(n_seq))]
    partners = []
    for a, b in all_shifts[:-1]:
        pz, px = lax.rem(z + a, n_dp), lax.rem(x + b, n_seq)
        partners.append((pz, px, pz * n_seq + px))

    barrier = pltpu.get_barrier_semaphore()
    for pz, px, _ in partners:
        pl.semaphore_signal(
            barrier, inc=1, device_id={"dp": pz, "seq": px}, device_id_type=MESH
        )

    offset = [offsets_ref[j] for j in range(pieces)]

    def group_with(shift):
        found = jnp.int32(0)
        for j in range(1, pieces):
            found = jnp.where(offset[j] == shift, jnp.int32(j), found)
        return found

    taken = [group_with(lax.rem(n - z + n_dp, n_dp)) for n in range(n_dp)]

    def stage(c):
        for n in range(n_dp):
            for s in range(n_seq):
                cols = slice((s * heads_each + c) * HD, (s * heads_each + c + 1) * HD)
                for i, ref in enumerate((q_ref, k_ref, v_ref, d_ref)):
                    send[c, n * n_seq + s, i] = ref[taken[n], :, cols]

    def send_copy(c, pz, px, m):
        return pltpu.make_async_remote_copy(
            src_ref=send.at[c, m],
            dst_ref=recv.at[c, me],
            send_sem=send_sem.at[c, m],
            recv_sem=recv_sem.at[c, me],
            device_id={"dp": pz, "seq": px},
            device_id_type=MESH,
        )

    def recv_copy(c, pz, px, m):
        return pltpu.make_async_remote_copy(
            src_ref=send.at[c, m],
            dst_ref=recv.at[c, m],
            send_sem=send_sem.at[c, m],
            recv_sem=recv_sem.at[c, m],
            device_id={"dp": pz, "seq": px},
            device_id_type=MESH,
        )

    def back_copy(c, pz, px, m):
        return pltpu.make_async_remote_copy(
            src_ref=back_send.at[c, m],
            dst_ref=back_recv[c].at[me],
            send_sem=back_send_sem.at[c, m],
            recv_sem=back_recv_sem.at[c, me],
            device_id={"dp": pz, "seq": px},
            device_id_type=MESH,
        )

    def back_arrival(c, pz, px, m):
        return pltpu.make_async_remote_copy(
            src_ref=back_send.at[c, m],
            dst_ref=back_recv[c].at[m],
            send_sem=back_send_sem.at[c, m],
            recv_sem=back_recv_sem.at[c, m],
            device_id={"dp": pz, "seq": px},
            device_id_type=MESH,
        )

    def loss_copy(step, mine):
        to = lax.rem(z + step, n_dp)
        slot = z if mine else to
        return pltpu.make_async_remote_copy(
            src_ref=loss_send,
            dst_ref=loss_recv.at[slot],
            send_sem=loss_send_sem.at[step],
            recv_sem=loss_recv_sem.at[slot],
            device_id={"dp": to},
            device_id_type=MESH,
        )

    loss_send[...] = jnp.zeros_like(loss_send)
    loss_send[0:1, 0:images] = losses_ref[...]
    loss_recv[z] = jnp.zeros(loss_send.shape, jnp.float32)
    loss_recv[z, 0:1, 0:images] = losses_ref[...]

    stage(0)
    pl.semaphore_wait(barrier, parts - 1)
    for step in range(1, n_dp):
        loss_copy(step, True).start()
    for c in range(heads_each):
        if c:
            stage(c)
        for pz, px, m in partners:
            send_copy(c, pz, px, m).start()

    for d in range(n_dp):
        shift = lax.rem(z - d + n_dp, n_dp)
        for s in range(n_seq):
            found = jnp.zeros((1, rows), jnp.int32)
            for j in range(pieces):
                at = (s * pieces + j) * rows
                found = found + jnp.where(
                    offset[j] == shift, segments_ref[0:1, at : at + rows], 0
                )
            m = d * n_seq + s
            ids_row[0:1, m * rows : (m + 1) * rows] = found.astype(jnp.float32)
    row_ids = ids_row[0:1, :]
    column_ids = jnp.transpose(jnp.broadcast_to(row_ids, (8, total)))[:, 0:1]

    for step in range(1, n_dp):
        loss_copy(step, False).wait_recv()
    loss_total = loss_recv[0]
    for d in range(1, n_dp):
        loss_total = loss_total + loss_recv[d]
    loss_mean = jnp.sum(loss_total) / (images * n_dp)
    image_weight = 2.0 / (1.0 + jnp.exp(losses_ref[...] - loss_mean))
    slots = lax.broadcasted_iota(jnp.int32, (total, images), 1).astype(jnp.float32)
    token_weight = jnp.sum(
        jnp.where(column_ids == slots, image_weight, 0.0), axis=1, keepdims=True
    )
    weight[...] = jnp.broadcast_to(token_weight, (total, HD))

    def work(c):
        recv[c, me] = send[c, me]
        for pz, px, m in partners:
            recv_copy(c, pz, px, m).wait_recv()
        q, k, v, d = (recv[c, :, i].reshape(total, HD) for i in range(4))
        d = (weight[...] * d.astype(jnp.float32)).astype(jnp.bfloat16)
        block = min(256, total)
        k_sum = v_sum = None
        per = block // rows
        for b in range(total // block):
            at = slice(b * block, (b + 1) * block)
            same = column_ids[at] == row_ids
            scores = jnp.where(same, dot_nt(q[at], k), -1e30)
            top = jnp.max(scores, axis=1, keepdims=True)
            e = jnp.exp2((scores - top) * (factor * log2e))
            p = e * (1.0 / jnp.sum(e, axis=1, keepdims=True))
            ga = dot_nt(d[at], v)
            inner = jnp.sum(p * ga, axis=1, keepdims=True)
            gs = (p * ((ga - inner) * factor)).astype(jnp.bfloat16)
            dq = jnp.dot(gs, k, preferred_element_type=jnp.float32).astype(jnp.bfloat16)
            back_send[c, b * per : (b + 1) * per, 0] = dq.reshape(per, rows, HD)
            k_part = dot_tn(gs, q[at])
            v_part = dot_tn(p.astype(jnp.bfloat16), d[at])
            k_sum = k_part if b == 0 else k_sum + k_part
            v_sum = v_part if b == 0 else v_sum + v_part
        back_send[c, :, 1] = k_sum.astype(jnp.bfloat16).reshape(parts, rows, HD)
        back_send[c, :, 2] = v_sum.astype(jnp.bfloat16).reshape(parts, rows, HD)

    for c in range(heads_each):
        work(c)
        for pz, px, m in partners:
            back_copy(c, pz, px, m).start()

    packs = [lax.rem(z + offset[j], n_dp) for j in range(pieces)]
    for c in range(heads_each):
        back_recv[c][me] = back_send[c, me]
        for pz, px, m in partners:
            back_arrival(c, pz, px, m).wait_recv()
        for s in range(n_seq):
            cols = slice((s * heads_each + c) * HD, (s * heads_each + c + 1) * HD)
            for j in range(pieces):
                for i, ref in enumerate((dq_ref, dk_ref, dv_ref)):
                    ref[j, :, cols] = back_recv[c][packs[j] * n_seq + s, i]

    for step in range(1, n_dp):
        loss_copy(step, True).wait_send()
    for c in range(heads_each):
        for pz, px, m in partners:
            send_copy(c, pz, px, m).wait_send()
            back_copy(c, pz, px, m).wait_send()


def kernel_shards(queries, key_vectors, value_rows, upstream, segments, losses, offsets):
    pieces, rows, columns = queries.shape[2:]
    n_dp = lax.axis_size("dp")
    n_seq = lax.axis_size("seq")
    heads_each = columns // (n_seq * HD)
    images = losses.shape[1]
    parts = n_dp * n_seq
    arrays = tuple(
        a.reshape(pieces, rows, columns) for a in (queries, key_vectors, value_rows, upstream)
    )
    whole = pl.BlockSpec(memory_space=pltpu.VMEM)
    result = jax.ShapeDtypeStruct((pieces, rows, columns), jnp.bfloat16)
    dma = pltpu.SemaphoreType.DMA
    grads = pl.pallas_call(
        functools.partial(exchange_kernel, n_dp, n_seq, pieces, rows, heads_each, images),
        out_shape=(result,) * 3,
        in_specs=[pl.BlockSpec(memory_space=pltpu.SMEM)] + [whole] * 6,
        out_specs=(whole,) * 3,
        scratch_shapes=[
            pltpu.VMEM((heads_each, parts, 4, rows, HD), jnp.bfloat16),
            pltpu.VMEM((heads_each, parts, 4, rows, HD), jnp.bfloat16),
            pltpu.VMEM((heads_each, parts, 3, rows, HD), jnp.bfloat16),
            pltpu.VMEM((8, 128), jnp.float32),
            pltpu.VMEM((n_dp, 8, 128), jnp.float32),
            pltpu.VMEM((8, parts * rows), jnp.float32),
            pltpu.VMEM((parts * rows, HD), jnp.float32),
        ]
        + [pltpu.VMEM((parts, 3, rows, HD), jnp.bfloat16)] * heads_each
        + [
            dma((heads_each, parts)),
            dma((heads_each, parts)),
            dma((heads_each, parts)),
            dma((heads_each, parts)),
            dma((n_dp,)),
            dma((n_dp,)),
        ],
        compiler_params=pltpu.CompilerParams(
            collective_id=0, has_side_effects=True, vmem_limit_bytes=48 * 1024 * 1024
        ),
    )(offsets, segments, losses, *arrays)
    return tuple(g.reshape(1, 1, pieces, rows, columns) for g in grads)


def shards(*arrays):
    rows = arrays[0].shape[3]
    partners = lax.axis_size("dp") * lax.axis_size("seq")
    if rows % 16 == 0 and partners <= 8:
        return kernel_shards(*arrays)
    return plain_shards(*arrays)


def solution(mesh):
    placed = (
        P("dp", "seq", None, None, "mp"),
        P("dp", "seq", None, None, "mp"),
        P("dp", "seq", None, None, "mp"),
        P("dp", "seq", None, None, "mp"),
        P("dp", None),
        P("dp", None),
        P(),
    )
    return jax.shard_map(
        shards,
        mesh=mesh,
        in_specs=placed,
        out_specs=(
            P("dp", "seq", None, None, "mp"),
            P("dp", "seq", None, None, "mp"),
            P("dp", "seq", None, None, "mp"),
        ),
        check_vma=False,
    )
```

```python
import functools
import math

import jax
import jax.numpy as jnp
from jax import lax
from jax.experimental import pallas as pl
from jax.experimental.pallas import tpu as pltpu
from jax.sharding import PartitionSpec as P

HD = 128


def for_sending(shard):

    def short(part):
        return part.astype(jnp.bfloat16) if part.dtype == jnp.float32 else part

    return jax.tree.map(short, shard)


def picked(block, slots):
    chosen = (slots[:, None] == jnp.arange(block.shape[0])[None, :]).astype(jnp.bfloat16)
    return jnp.einsum("jn,nrc->jrc", chosen, block, preferred_element_type=jnp.float32).astype(
        jnp.bfloat16
    )


def softmax_grads(q_rows, k_rows, v_rows, d_rows, image_ids):
    total_rows = q_rows.shape[0]
    block_rows = min(512, total_rows)
    factor = q_rows.shape[1] ** (-0.5)
    key_total = jnp.zeros(k_rows.shape, jnp.float32)
    value_total = jnp.zeros(v_rows.shape, jnp.float32)
    query_pieces = []
    for start_row in range(0, total_rows, block_rows):
        q_block = q_rows[start_row : start_row + block_rows]
        d_block = d_rows[start_row : start_row + block_rows]
        same_image = image_ids[start_row : start_row + block_rows, None] == image_ids[None, :]
        scores = (
            jnp.einsum("td,ud->tu", q_block, k_rows, preferred_element_type=jnp.float32) * factor
        )
        masked = jnp.where(same_image, scores, -1e30)
        row_top = jnp.max(masked, axis=1, keepdims=True)
        exponent = jnp.exp(masked - row_top)
        attention = exponent / jnp.sum(exponent, axis=1, keepdims=True)
        grad_attention = jnp.einsum(
            "td,ud->tu", d_block, v_rows, preferred_element_type=jnp.float32
        )
        row_inner = jnp.sum(attention * grad_attention, axis=1, keepdims=True)
        grad_scores = (attention * (grad_attention - row_inner) * factor).astype(jnp.bfloat16)
        query_pieces.append(
            jnp.einsum("tu,ud->td", grad_scores, k_rows, preferred_element_type=jnp.float32).astype(
                jnp.bfloat16
            )
        )
        key_total = key_total + jnp.einsum(
            "tu,td->ud", grad_scores, q_block, preferred_element_type=jnp.float32
        )
        value_total = value_total + jnp.einsum(
            "tu,td->ud", attention.astype(jnp.bfloat16), d_block, preferred_element_type=jnp.float32
        )
    return (
        jnp.concatenate(query_pieces, axis=0),
        key_total.astype(jnp.bfloat16),
        value_total.astype(jnp.bfloat16),
    )


def plain_shards(queries, key_vectors, value_rows, upstream, segments, losses, offsets):
    pieces = queries.shape[2]
    piece_rows = queries.shape[3]
    columns = queries.shape[4]
    local_rows = pieces * piece_rows
    dp_count = lax.axis_size("dp")
    seq_count = lax.axis_size("seq")
    position = lax.axis_index("dp")
    dp_slots = jnp.arange(dp_count, dtype=jnp.int32)
    loss_sum = lax.psum(jnp.sum(losses), "dp")
    loss_mean = loss_sum / (losses.shape[1] * dp_count)
    image_weight = 2.0 / (1.0 + jnp.exp(losses[0] - loss_mean))
    image_ids = segments[0]
    image_slots = jnp.arange(losses.shape[1], dtype=jnp.int32)
    token_weight = jnp.sum(
        jnp.where(image_ids[:, None] == image_slots[None, :], image_weight[None, :], 0.0), axis=1
    )
    local_parts = tuple(
        (
            array.reshape(pieces, piece_rows, columns)
            for array in (queries, key_vectors, value_rows, upstream)
        )
    )
    targets = (position + offsets) % dp_count
    select = (targets[None, :] == dp_slots[:, None]).astype(jnp.bfloat16)
    outgoing = tuple(
        (
            jnp.einsum("nj,jrc->nrc", select, block, preferred_element_type=jnp.float32).astype(
                jnp.bfloat16
            )
            for block in local_parts
        )
    )
    incoming = (
        lax.all_to_all(outgoing[0], "dp", split_axis=0, concat_axis=0, tiled=True),
        lax.all_to_all(outgoing[1], "dp", split_axis=0, concat_axis=0, tiled=True),
        lax.all_to_all(outgoing[2], "dp", split_axis=0, concat_axis=0, tiled=True),
        lax.all_to_all(outgoing[3], "dp", split_axis=0, concat_axis=0, tiled=True),
    )
    sources = (position - offsets) % dp_count
    arrived = tuple((picked(block, sources) for block in incoming))
    heads_each = columns // (seq_count * HD)
    grouped = tuple((block.reshape(local_rows, seq_count, heads_each, HD) for block in arrived))
    q_all = lax.all_to_all(grouped[0], "seq", split_axis=1, concat_axis=0, tiled=True)[:, 0]
    k_all = lax.all_to_all(grouped[1], "seq", split_axis=1, concat_axis=0, tiled=True)[:, 0]
    v_all = lax.all_to_all(grouped[2], "seq", split_axis=1, concat_axis=0, tiled=True)[:, 0]
    grad_out = (
        token_weight[:, None, None]
        * lax.all_to_all(grouped[3], "seq", split_axis=1, concat_axis=0, tiled=True)[:, 0].astype(
            jnp.float32
        )
    ).astype(jnp.bfloat16)
    grads = jax.vmap(softmax_grads, in_axes=(1, 1, 1, 1, None), out_axes=1)(
        q_all, k_all, v_all, grad_out, image_ids
    )
    results = tuple((item[:, None] for item in grads))
    returned = (
        lax.all_to_all(for_sending(results[0]), "seq", split_axis=0, concat_axis=1, tiled=True),
        lax.all_to_all(for_sending(results[1]), "seq", split_axis=0, concat_axis=1, tiled=True),
        lax.all_to_all(for_sending(results[2]), "seq", split_axis=0, concat_axis=1, tiled=True),
    )
    back_parts = tuple((block.reshape(pieces, piece_rows, columns) for block in returned))
    anchors = (position - offsets) % dp_count
    select_back = (anchors[None, :] == dp_slots[:, None]).astype(jnp.bfloat16)
    outgoing_back = tuple(
        (
            jnp.einsum(
                "nj,jrc->nrc", select_back, block, preferred_element_type=jnp.float32
            ).astype(jnp.bfloat16)
            for block in back_parts
        )
    )
    incoming_back = (
        lax.all_to_all(outgoing_back[0], "dp", split_axis=0, concat_axis=0, tiled=True),
        lax.all_to_all(outgoing_back[1], "dp", split_axis=0, concat_axis=0, tiled=True),
        lax.all_to_all(outgoing_back[2], "dp", split_axis=0, concat_axis=0, tiled=True),
    )
    destinations = (position + offsets) % dp_count
    finished = tuple((picked(block, destinations) for block in incoming_back))
    return tuple((block.reshape(1, 1, pieces, piece_rows, columns) for block in finished))


MESH = pl.DeviceIdType.MESH


def dot_nt(a, b):
    return lax.dot_general(a, b, (((1,), (1,)), ((), ())), preferred_element_type=jnp.float32)


def dot_tn(a, b):
    return lax.dot_general(a, b, (((0,), (0,)), ((), ())), preferred_element_type=jnp.float32)


def exchange_kernel(
    n_dp,
    n_seq,
    pieces,
    rows,
    heads_each,
    images,
    offsets_ref,
    segments_ref,
    losses_ref,
    q_ref,
    k_ref,
    v_ref,
    d_ref,
    arrived_ref,
    *scratch,
):
    send, recv, back_send, loss_send, loss_recv, ids_row, weight = scratch[:7]
    loaded = scratch[7 : 7 + heads_each]
    (load_sem, send_sem, recv_sem, back_send_sem, back_recv_sem, loss_send_sem, loss_recv_sem) = (
        scratch[7 + heads_each :]
    )
    z = lax.axis_index("dp")
    x = lax.axis_index("seq")
    me = z * n_seq + x
    parts = n_dp * n_seq
    total = parts * rows
    factor = HD**-0.5
    log2e = math.log2(math.e)

    dp_shifts = sorted(range(n_dp), key=lambda s: -min(s, n_dp - s))
    all_shifts = [(a, b) for a in dp_shifts for b in reversed(range(n_seq))]
    partners = []
    for a, b in all_shifts[:-1]:
        pz, px = lax.rem(z + a, n_dp), lax.rem(x + b, n_seq)
        partners.append((pz, px, pz * n_seq + px))

    def columns_of(s, c):
        return pl.ds(pl.multiple_of((s * heads_each + c) * HD, HD), HD)

    def loads(c):
        return [
            pltpu.make_async_copy(
                ref.at[:, :, columns_of(s, c)], loaded[c].at[s, i], load_sem.at[c, s, i]
            )
            for s in range(n_seq)
            for i, ref in enumerate((q_ref, k_ref, v_ref, d_ref))
        ]

    for c in range(heads_each):
        for load in loads(c):
            load.start()

    barrier = pltpu.get_barrier_semaphore()
    for pz, px, _ in partners:
        pl.semaphore_signal(
            barrier, inc=1, device_id={"dp": pz, "seq": px}, device_id_type=MESH
        )

    offset = [offsets_ref[j] for j in range(pieces)]

    def group_with(shift):
        found = jnp.int32(0)
        for j in range(1, pieces):
            found = jnp.where(offset[j] == shift, jnp.int32(j), found)
        return found

    taken = [group_with(lax.rem(n - z + n_dp, n_dp)) for n in range(n_dp)]

    def stage(c):
        for load in loads(c):
            load.wait()
        for n in range(n_dp):
            for s in range(n_seq):
                for i in range(4):
                    send[c, n * n_seq + s, i] = loaded[c][s, i, taken[n]]

    def send_copy(c, pz, px, m):
        return pltpu.make_async_remote_copy(
            src_ref=send.at[c, m],
            dst_ref=recv.at[c, me],
            send_sem=send_sem.at[c, m],
            recv_sem=recv_sem.at[c, me],
            device_id={"dp": pz, "seq": px},
            device_id_type=MESH,
        )

    def recv_copy(c, pz, px, m):
        return pltpu.make_async_remote_copy(
            src_ref=send.at[c, m],
            dst_ref=recv.at[c, m],
            send_sem=send_sem.at[c, m],
            recv_sem=recv_sem.at[c, m],
            device_id={"dp": pz, "seq": px},
            device_id_type=MESH,
        )

    def back_copy(c, pz, px, m):
        return pltpu.make_async_remote_copy(
            src_ref=back_send.at[c, m],
            dst_ref=arrived_ref.at[:, z, :, columns_of(x, c)],
            send_sem=back_send_sem.at[c, m],
            recv_sem=back_recv_sem.at[c, me],
            device_id={"dp": pz, "seq": px},
            device_id_type=MESH,
        )

    def kept_copy(c):
        return pltpu.make_async_copy(
            back_send.at[c, me],
            arrived_ref.at[:, z, :, columns_of(x, c)],
            back_recv_sem.at[c, me],
        )

    def back_arrival(c, pz, px, m):
        return pltpu.make_async_remote_copy(
            src_ref=back_send.at[c, m],
            dst_ref=arrived_ref.at[:, pz, :, columns_of(px, c)],
            send_sem=back_send_sem.at[c, m],
            recv_sem=back_recv_sem.at[c, m],
            device_id={"dp": pz, "seq": px},
            device_id_type=MESH,
        )

    def loss_copy(step, mine):
        to = lax.rem(z + step, n_dp)
        slot = z if mine else to
        return pltpu.make_async_remote_copy(
            src_ref=loss_send,
            dst_ref=loss_recv.at[slot],
            send_sem=loss_send_sem.at[step],
            recv_sem=loss_recv_sem.at[slot],
            device_id={"dp": to},
            device_id_type=MESH,
        )

    loss_send[...] = jnp.zeros_like(loss_send)
    loss_send[0:1, 0:images] = losses_ref[...]
    loss_recv[z] = jnp.zeros(loss_send.shape, jnp.float32)
    loss_recv[z, 0:1, 0:images] = losses_ref[...]

    stage(0)
    pl.semaphore_wait(barrier, parts - 1)
    for step in range(1, n_dp):
        loss_copy(step, True).start()
    for c in range(heads_each):
        if c:
            stage(c)
        for pz, px, m in partners:
            send_copy(c, pz, px, m).start()

    for d in range(n_dp):
        shift = lax.rem(z - d + n_dp, n_dp)
        for s in range(n_seq):
            found = jnp.zeros((1, rows), jnp.int32)
            for j in range(pieces):
                at = (s * pieces + j) * rows
                found = found + jnp.where(
                    offset[j] == shift, segments_ref[0:1, at : at + rows], 0
                )
            m = d * n_seq + s
            ids_row[0:1, m * rows : (m + 1) * rows] = found.astype(jnp.float32)
    row_ids = ids_row[0:1, :]
    column_ids = jnp.transpose(jnp.broadcast_to(row_ids, (8, total)))[:, 0:1]

    for step in range(1, n_dp):
        loss_copy(step, False).wait_recv()
    loss_total = loss_recv[0]
    for d in range(1, n_dp):
        loss_total = loss_total + loss_recv[d]
    loss_mean = jnp.sum(loss_total) / (images * n_dp)
    image_weight = 2.0 / (1.0 + jnp.exp(losses_ref[...] - loss_mean))
    slots = lax.broadcasted_iota(jnp.int32, (total, images), 1).astype(jnp.float32)
    token_weight = jnp.sum(
        jnp.where(column_ids == slots, image_weight, 0.0), axis=1, keepdims=True
    )
    weight[...] = jnp.broadcast_to(token_weight, (total, HD))

    def work(c):
        recv[c, me] = send[c, me]
        for pz, px, m in partners:
            recv_copy(c, pz, px, m).wait_recv()
        q, k, v, d = (recv[c, :, i].reshape(total, HD) for i in range(4))
        d = (weight[...] * d.astype(jnp.float32)).astype(jnp.bfloat16)
        block = min(256, total)
        k_sum = v_sum = None
        per = block // rows
        for b in range(total // block):
            at = slice(b * block, (b + 1) * block)
            same = column_ids[at] == row_ids
            scores = jnp.where(same, dot_nt(q[at], k), -1e30)
            top = jnp.max(scores, axis=1, keepdims=True)
            e = jnp.exp2((scores - top) * (factor * log2e))
            p = e * (1.0 / jnp.sum(e, axis=1, keepdims=True))
            ga = dot_nt(d[at], v)
            inner = jnp.sum(p * ga, axis=1, keepdims=True)
            gs = (p * ((ga - inner) * factor)).astype(jnp.bfloat16)
            dq = jnp.dot(gs, k, preferred_element_type=jnp.float32).astype(jnp.bfloat16)
            back_send[c, b * per : (b + 1) * per, 0] = dq.reshape(per, rows, HD)
            k_part = dot_tn(gs, q[at])
            v_part = dot_tn(p.astype(jnp.bfloat16), d[at])
            k_sum = k_part if b == 0 else k_sum + k_part
            v_sum = v_part if b == 0 else v_sum + v_part
        back_send[c, :, 1] = k_sum.astype(jnp.bfloat16).reshape(parts, rows, HD)
        back_send[c, :, 2] = v_sum.astype(jnp.bfloat16).reshape(parts, rows, HD)

    for c in range(heads_each):
        work(c)
        for pz, px, m in partners:
            back_copy(c, pz, px, m).start()
        kept_copy(c).start()

    for c in range(heads_each):
        for pz, px, m in partners:
            back_arrival(c, pz, px, m).wait_recv()
        kept_copy(c).wait()

    for step in range(1, n_dp):
        loss_copy(step, True).wait_send()
    for c in range(heads_each):
        for pz, px, m in partners:
            send_copy(c, pz, px, m).wait_send()
            back_copy(c, pz, px, m).wait_send()


def order_kernel(n_dp, pieces, offsets_ref, arrived_ref, dq_ref, dk_ref, dv_ref, held, in_sem, out_sem):
    z = lax.axis_index("dp")
    into, out = [], []
    for j in range(pieces):
        pack = lax.rem(z + offsets_ref[j], n_dp)
        for i, ref in enumerate((dq_ref, dk_ref, dv_ref)):
            into.append(
                pltpu.make_async_copy(arrived_ref.at[i, pack], held.at[i, j], in_sem.at[i, j])
            )
            out.append(pltpu.make_async_copy(held.at[i, j], ref.at[j], out_sem.at[i, j]))
    for copy in into:
        copy.start()
    for copy, after in zip(into, out):
        copy.wait()
        after.start()
    for after in out:
        after.wait()


def kernel_shards(queries, key_vectors, value_rows, upstream, segments, losses, offsets):
    pieces, rows, columns = queries.shape[2:]
    n_dp = lax.axis_size("dp")
    n_seq = lax.axis_size("seq")
    heads_each = columns // (n_seq * HD)
    images = losses.shape[1]
    parts = n_dp * n_seq
    arrays = tuple(
        a.reshape(pieces, rows, columns) for a in (queries, key_vectors, value_rows, upstream)
    )
    whole = pl.BlockSpec(memory_space=pltpu.VMEM)
    result = jax.ShapeDtypeStruct((pieces, rows, columns), jnp.bfloat16)
    dma = pltpu.SemaphoreType.DMA
    arrived = pl.pallas_call(
        functools.partial(exchange_kernel, n_dp, n_seq, pieces, rows, heads_each, images),
        out_shape=jax.ShapeDtypeStruct((3, n_dp, rows, columns), jnp.bfloat16),
        in_specs=[pl.BlockSpec(memory_space=pltpu.SMEM)]
        + [whole] * 2
        + [pl.BlockSpec(memory_space=pl.ANY)] * 4,
        out_specs=pl.BlockSpec(memory_space=pl.ANY),
        scratch_shapes=[
            pltpu.VMEM((heads_each, parts, 4, rows, HD), jnp.bfloat16),
            pltpu.VMEM((heads_each, parts, 4, rows, HD), jnp.bfloat16),
            pltpu.VMEM((heads_each, parts, 3, rows, HD), jnp.bfloat16),
            pltpu.VMEM((8, 128), jnp.float32),
            pltpu.VMEM((n_dp, 8, 128), jnp.float32),
            pltpu.VMEM((8, parts * rows), jnp.float32),
            pltpu.VMEM((parts * rows, HD), jnp.float32),
        ]
        + [pltpu.VMEM((n_seq, 4, pieces, rows, HD), jnp.bfloat16)] * heads_each
        + [
            dma((heads_each, n_seq, 4)),
            dma((heads_each, parts)),
            dma((heads_each, parts)),
            dma((heads_each, parts)),
            dma((heads_each, parts)),
            dma((n_dp,)),
            dma((n_dp,)),
        ],
        compiler_params=pltpu.CompilerParams(
            collective_id=0, has_side_effects=True, vmem_limit_bytes=56 * 1024 * 1024
        ),
    )(offsets, segments, losses, *arrays)
    grads = pl.pallas_call(
        functools.partial(order_kernel, n_dp, pieces),
        out_shape=(result,) * 3,
        in_specs=[pl.BlockSpec(memory_space=pltpu.SMEM), pl.BlockSpec(memory_space=pl.ANY)],
        out_specs=(pl.BlockSpec(memory_space=pl.ANY),) * 3,
        scratch_shapes=[
            pltpu.VMEM((3, pieces, rows, columns), jnp.bfloat16),
            dma((3, pieces)),
            dma((3, pieces)),
        ],
        compiler_params=pltpu.CompilerParams(vmem_limit_bytes=56 * 1024 * 1024),
    )(offsets, arrived)
    return tuple(g.reshape(1, 1, pieces, rows, columns) for g in grads)


def shards(*arrays):
    rows = arrays[0].shape[3]
    partners = lax.axis_size("dp") * lax.axis_size("seq")
    if rows % 16 == 0 and partners <= 8:
        return kernel_shards(*arrays)
    return plain_shards(*arrays)


def solution(mesh):
    placed = (
        P("dp", "seq", None, None, "mp"),
        P("dp", "seq", None, None, "mp"),
        P("dp", "seq", None, None, "mp"),
        P("dp", "seq", None, None, "mp"),
        P("dp", None),
        P("dp", None),
        P(),
    )
    return jax.shard_map(
        shards,
        mesh=mesh,
        in_specs=placed,
        out_specs=(
            P("dp", "seq", None, None, "mp"),
            P("dp", "seq", None, None, "mp"),
            P("dp", "seq", None, None, "mp"),
        ),
        check_vma=False,
    )
```
